512 devices in a mesh: dp: 8 (over y_lo, x), pipe: 4 (over y_hi, core), tensor: 16 (over z).
Axes of the slice: x: 4, y: 4 (y_hi: 2, y_lo: 2; y = y_hi * 2 + y_lo), z: 16, core: 2. Of those that a mesh axis runs over, the one named last changes fastest.
Arguments:
- saved_input: bfloat16 [8, 4, 1024, 1536], P('dp', 'pipe', 'tensor'), may hold values from -6 to 6
- grad_in: bfloat16 [8, 4, 1024, 1536], P('dp', 'pipe', 'tensor'), may hold values from -6 to 6
- segment_ids: int32 [8, 4, 1024], P('dp', 'pipe'), may hold values from 0 to 7, never falling along the last dimension, each value on 1 to 256 neighbouring positions
- w_qkv: bfloat16 [4, 1536, 16, 384], P('pipe', 'dp', 'tensor'), may hold values from -0.15625 to 0.15625
- w_out: bfloat16 [4, 16, 128, 1536], P('pipe', 'tensor', 'dp'), may hold values from -0.125 to 0.125
- q_gain: float32 [4, 128], P('pipe'), may hold values from 0.5 to 1.5
- k_gain: float32 [4, 128], P('pipe'), may hold values from 0.5 to 1.5
Outputs:
- grad_out: bfloat16 [8, 4, 1024, 1536], P('dp', 'pipe', 'tensor')
- grad_qkv: bfloat16 [4, 1536, 16, 384], P('pipe', None, 'tensor')
- grad_wout: bfloat16 [4, 16, 128, 1536], P('pipe', 'tensor')
The draws below stay inside these ranges and needn't reach their ends.
Inputs may be any that keep to these rules, and one draw needn't show every extreme that they name: `segment_ids`: in each micro-batch the ids never fall along the tokens; every id 0 to 7 occurs, on 1 to 256 tokens, and one clip has exactly 256.
All inputs are finite; a program needn't handle non-finite values.
Results may differ from the reference program's by a relative error of at most 0.019.
Values may be sent and summed in bfloat16 or wider, within the bound.
No kernel may reach another device: no remote copies, remote signals or barrier semaphores. Data moves between devices by JAX's collectives and lax.ppermute only.
A program may use at most 64 MiB of HBM per device.

```python
import math
import jax
import jax.numpy as jnp
import numpy as np
from jax import lax

D = 1536
HD = 128
SEGS = 8
HEADS = 16
SEQ = 1024
N_DP = 8
N_PIPE = 4


def block_levels(own_key, extent, shards, low, top_value):
    loudness, own = 1.0, jax.random.fold_in(own_key, 6)
    for axis_at, blocks in shards:
        steps = jnp.exp(jax.random.uniform(jax.random.fold_in(own, axis_at), (blocks,), jnp.float32, low / len(shards), top_value / len(shards)))
        loudness = loudness * jnp.repeat(steps, extent[axis_at] // blocks).reshape([-1 if axis == axis_at else 1 for axis in range(len(extent))])
    return loudness


def split_up(number_of, total, limit, lean):
    weights = [(1 << 20) // math.isqrt(standing ** lean) + 1 for standing in range(2, number_of + 1)]
    surplus, given = total - limit - (number_of - 1), [1] * (number_of - 1)
    while surplus > 0:
        movable = [i for i in range(number_of - 1) if given[i] < limit]
        mass, budget = sum([weights[i] for i in movable]), surplus
        for i in movable:
            addition = min(limit - given[i], max(1, budget * weights[i] // mass), surplus)
            given[i] = given[i] + addition
            surplus = surplus - addition
    return np.array([limit] + given)


def uneven(key, amount, total, most, slope):
    if amount == 2:
        one = jax.random.randint(key, (), max(1, total - most), min(most, total - 1) + 1)
        return jnp.stack([one, total - one])
    tallies = jnp.asarray(split_up(amount, total, most, slope), jnp.int32)
    pairs = (amount - 1) // 2
    source_of, receiver = tallies[1:1 + 2 * pairs:2], tallies[2:2 + 2 * pairs:2]
    margin = jnp.minimum(source_of - 1, most - receiver)
    moved = jax.random.randint(jax.random.fold_in(key, 1), (pairs,), 0, 1 << 20) % (margin + 1)
    tallies = tallies.at[1:1 + 2 * pairs:2].set(source_of - moved).at[2:2 + 2 * pairs:2].set(receiver + moved)
    return tallies[jax.random.permutation(jax.random.fold_in(key, 2), amount)]


def gaussian(key, shape, scale, limit, split=(), kind=jnp.bfloat16):
    entries = scale * jax.random.normal(key, shape, jnp.float32)
    if split:
        entries = entries * block_levels(key, shape, split, -0.22, 0.18)
    return jnp.clip(entries, -limit, limit).astype(kind)


def setup_inputs(seed: int = 0) -> dict:
    arg_keys = jax.random.split(jax.random.key(seed), 8)
    saved_input = gaussian(arg_keys[0], (N_DP, N_PIPE, SEQ, D), 1.0, 6.0, ((0, 8), (1, 4), (2, 16)))
    grad_in = gaussian(arg_keys[1], (N_DP, N_PIPE, SEQ, D), 1.0, 6.0, ((0, 8), (1, 4), (2, 16)))
    segment_ids = jax.vmap(lambda own: jnp.searchsorted(jnp.cumsum(uneven(own, SEGS, SEQ, SEQ // 4, 2)), jnp.arange(SEQ), side="right"))(jax.random.split(arg_keys[2], N_DP * N_PIPE)).reshape((N_DP, N_PIPE, SEQ)).astype(jnp.int32)
    w_qkv = gaussian(arg_keys[3], (N_PIPE, D, HEADS, 3 * HD), D ** -0.5, 0.15625, ((0, 4), (1, 8), (2, 16)))
    w_out = gaussian(arg_keys[4], (N_PIPE, HEADS, HD, D), (HEADS * HD) ** -0.5, 0.125, ((0, 4), (1, 16), (2, 8)))
    q_gain = jnp.clip(1.0 + 0.1 * jax.random.normal(arg_keys[5], (N_PIPE, HD), jnp.float32), 0.5, 1.5)
    k_gain = jnp.clip(1.0 + 0.1 * jax.random.normal(arg_keys[6], (N_PIPE, HD), jnp.float32), 0.5, 1.5)
    return dict(saved_input=saved_input, grad_in=grad_in, segment_ids=segment_ids, w_qkv=w_qkv, w_out=w_out, q_gain=q_gain, k_gain=k_gain)


EPS = 1e-06

def head_backward(normed, cotangent, same_segment, proj, outw, q_scale, k_scale):
    width = proj.shape[1] // 3
    factor = width ** (-0.5)
    joined = jnp.dot(normed, proj, preferred_element_type=jnp.float32)
    query = joined[:, :width]
    keys = joined[:, width:2 * width]
    values = joined[:, 2 * width:]
    q_rate = lax.rsqrt(lax.optimization_barrier(jnp.mean(query * query, axis=-1, keepdims=True)) + EPS)
    q_unit = query * q_rate
    q_norm = (q_unit * q_scale).astype(jnp.bfloat16)
    k_rate = lax.rsqrt(lax.optimization_barrier(jnp.mean(keys * keys, axis=-1, keepdims=True)) + EPS)
    k_unit = keys * k_rate
    k_norm = (k_unit * k_scale).astype(jnp.bfloat16)
    v_low = values.astype(jnp.bfloat16)
    scores = jnp.dot(q_norm, k_norm.T, preferred_element_type=jnp.float32) * factor
    expd = jnp.exp(scores) * same_segment
    probs = expd / lax.optimization_barrier(jnp.sum(expd, axis=-1, keepdims=True))
    probs_low = probs.astype(jnp.bfloat16)
    attended = jnp.dot(probs_low, v_low, preferred_element_type=jnp.float32).astype(jnp.bfloat16)
    d_attended = jnp.dot(cotangent, outw.T, preferred_element_type=jnp.float32).astype(jnp.bfloat16)
    d_outw = jnp.dot(attended.T, cotangent, preferred_element_type=jnp.float32)
    d_probs = jnp.dot(d_attended, v_low.T, preferred_element_type=jnp.float32)
    d_values = jnp.dot(probs_low.T, d_attended, preferred_element_type=jnp.float32)
    row_delta = lax.optimization_barrier(jnp.sum(probs * d_probs, axis=-1, keepdims=True))
    d_scores = (probs * (d_probs - row_delta) * factor).astype(jnp.bfloat16)
    d_qnorm = jnp.dot(d_scores, k_norm, preferred_element_type=jnp.float32)
    d_knorm = jnp.dot(d_scores.T, q_norm, preferred_element_type=jnp.float32)
    q_back = d_qnorm * q_scale
    d_query = q_rate * (q_back - q_unit * lax.optimization_barrier(jnp.mean(q_back * q_unit, axis=-1, keepdims=True)))
    k_back = d_knorm * k_scale
    d_keys = k_rate * (k_back - k_unit * lax.optimization_barrier(jnp.mean(k_back * k_unit, axis=-1, keepdims=True)))
    d_joined = jnp.concatenate([d_query, d_keys, d_values], axis=-1).astype(jnp.bfloat16)
    d_proj = jnp.dot(normed.T, d_joined, preferred_element_type=jnp.float32)
    term = jnp.dot(d_joined, proj.T, preferred_element_type=jnp.float32).astype(jnp.bfloat16)
    term = lax.optimization_barrier(term).astype(jnp.float32)
    return (term, d_proj, d_outw)

def section_backward(tokens, cotangent, segments, proj_all, out_all, q_scale, k_scale):
    x_float = tokens.astype(jnp.float32)
    centred = x_float - lax.optimization_barrier(jnp.mean(x_float, axis=-1, keepdims=True))
    scaled = lax.rsqrt(lax.optimization_barrier(jnp.mean(centred * centred, axis=-1, keepdims=True)) + EPS)
    unit = centred * scaled
    normed = unit.astype(jnp.bfloat16)
    same_segment = (segments[:, None] == segments[None, :]).astype(jnp.float32)
    proj_heads = jnp.transpose(proj_all, (1, 0, 2))

    def per_head(total, item):
        proj, outw = item
        term, d_proj, d_outw = head_backward(normed, cotangent, same_segment, proj, outw, q_scale, k_scale)
        return (total + term, (d_proj, d_outw))
    start = jnp.zeros(tokens.shape, jnp.float32)
    d_normed, grads = lax.scan(per_head, start, (proj_heads, out_all))
    d_proj, d_outw = grads
    d_tokens = cotangent.astype(jnp.float32) + scaled * (d_normed - lax.optimization_barrier(jnp.mean(d_normed, axis=-1, keepdims=True)) - unit * lax.optimization_barrier(jnp.mean(d_normed * unit, axis=-1, keepdims=True)))
    return (d_tokens.astype(jnp.bfloat16), jnp.transpose(d_proj, (1, 0, 2)), d_outw)

def reference(saved_input, grad_in, segment_ids, w_qkv, w_out, q_gain, k_gain):
    token_grads = []
    proj_grads = []
    out_grads = []
    for section_number in range(N_PIPE):

        def micro_step(carry, item):
            tokens, cotangent, segments = item
            d_tokens, d_proj, d_outw = section_backward(tokens, cotangent, segments, w_qkv[section_number], w_out[section_number], q_gain[section_number], k_gain[section_number])
            proj_sum = carry[0] + lax.optimization_barrier(d_proj.astype(jnp.bfloat16)).astype(jnp.float32)
            out_sum = carry[1] + lax.optimization_barrier(d_outw.astype(jnp.bfloat16)).astype(jnp.float32)
            return ((proj_sum, out_sum), d_tokens)
        start = (jnp.zeros(w_qkv.shape[1:], jnp.float32), jnp.zeros(w_out.shape[1:], jnp.float32))
        sums, d_all = lax.scan(micro_step, start, (saved_input[:, section_number], grad_in[:, section_number], segment_ids[:, section_number]))
        token_grads.append(d_all)
        proj_grads.append(sums[0].astype(jnp.bfloat16))
        out_grads.append(sums[1].astype(jnp.bfloat16))
    stacked = jnp.stack(token_grads, axis=1)
    grad_out = jnp.roll(stacked, -1, axis=1)
    return (grad_out, jnp.stack(proj_grads, axis=0), jnp.stack(out_grads, axis=0))
```

```python
import jax
import jax.numpy as jnp
from jax import lax
from jax.sharding import PartitionSpec as P

EPS = 1e-06


def shifted(array, axis, by):
    peers = lax.axis_size(axis)
    return lax.ppermute(array, axis, [(i, (i + by) % peers) for i in range(peers)])


def contract(left, right, left_dim, right_dim):
    return lax.dot_general(
        left, right, (((left_dim,), (right_dim,)), ((), ())), preferred_element_type=jnp.float32
    )


def ring_gather(block, axis):
    peers = lax.axis_size(axis)
    got = {0: block}
    up = down = block
    for step in range(1, peers // 2 + 1):
        up = shifted(up, axis, 1)
        got[peers - step] = up
        if step < peers - step:
            down = shifted(down, axis, -1)
            got[step] = down
    return [got[i] for i in range(peers)]


def fold_wide(wide, parts, width):
    rows, cols = wide.shape
    cut = [wide[:, c : c + width].reshape(parts, rows // parts, width) for c in range(0, cols, width)]
    return jnp.concatenate(cut, axis=1)


def unfold_wide(folded, cols):
    parts, rows, width = folded.shape
    high = rows * width // cols
    cut = [folded[:, i * high : (i + 1) * high].reshape(parts * high, width) for i in range(cols // width)]
    return jnp.concatenate(cut, axis=1)


def per_device(saved_input, grad_in, segment_ids, w_qkv, w_out, q_gain, k_gain):
    dp = lax.axis_size("dp")
    me = lax.axis_index("tensor")
    x_float = saved_input[0, 0].astype(jnp.float32)
    rows = x_float.shape[0]
    centred = x_float - jnp.mean(x_float, axis=-1, keepdims=True)
    scaled = lax.rsqrt(jnp.mean(centred * centred, axis=-1, keepdims=True) + EPS)
    unit = centred * scaled
    cot_rows = grad_in[0, 0]
    three = w_qkv.shape[3]
    share = w_qkv.shape[1]
    weights = jnp.concatenate([w_qkv[0, :, 0, :], fold_wide(w_out[0, 0], 1, three)[0]], axis=0)
    weights = lax.all_gather(weights, "dp", axis=0)
    proj_full = weights[:, :share].reshape(dp * share, three)
    outw_full = unfold_wide(weights[:, share:], w_out.shape[3])
    blocks = ring_gather(jnp.concatenate([unit.astype(jnp.bfloat16), cot_rows], axis=0), "tensor")
    normed = jnp.concatenate([b[:rows] for b in blocks], axis=0)
    cotangent = jnp.concatenate([b[rows:] for b in blocks], axis=0)
    tokens = normed.shape[0]
    width = outw_full.shape[0]
    factor = width ** (-0.5)
    q_scale = q_gain[0]
    k_scale = k_gain[0]
    segments = segment_ids[0, 0]
    segments = lax.dynamic_slice(jnp.concatenate([segments, segments]), (me * rows,), (tokens,))
    same_segment = (segments[:, None] == segments[None, :]).astype(jnp.float32)
    joined = jnp.dot(normed, proj_full, preferred_element_type=jnp.float32)
    query = joined[:, :width]
    keys = joined[:, width : 2 * width]
    values = joined[:, 2 * width :]
    q_rate = lax.rsqrt(jnp.mean(query * query, axis=-1, keepdims=True) + EPS)
    q_unit = query * q_rate
    q_norm = (q_unit * q_scale).astype(jnp.bfloat16)
    k_rate = lax.rsqrt(jnp.mean(keys * keys, axis=-1, keepdims=True) + EPS)
    k_unit = keys * k_rate
    k_norm = (k_unit * k_scale).astype(jnp.bfloat16)
    v_low = values.astype(jnp.bfloat16)
    scores = contract(q_norm, k_norm, 1, 1) * factor
    expd = jnp.exp(scores) * same_segment
    probs = expd / jnp.sum(expd, axis=-1, keepdims=True)
    probs_low = probs.astype(jnp.bfloat16)
    attended = jnp.dot(probs_low, v_low, preferred_element_type=jnp.float32).astype(jnp.bfloat16)
    d_attended = contract(cotangent, outw_full, 1, 1).astype(jnp.bfloat16)
    d_outw = contract(attended, cotangent, 0, 0)
    d_probs = contract(d_attended, v_low, 1, 1)
    d_values = contract(probs_low, d_attended, 0, 0)
    row_delta = jnp.sum(probs * d_probs, axis=-1, keepdims=True)
    d_scores = (probs * (d_probs - row_delta) * factor).astype(jnp.bfloat16)
    d_qnorm = jnp.dot(d_scores, k_norm, preferred_element_type=jnp.float32)
    d_knorm = contract(d_scores, q_norm, 0, 0)
    q_back = d_qnorm * q_scale
    d_query = q_rate * (q_back - q_unit * jnp.mean(q_back * q_unit, axis=-1, keepdims=True))
    k_back = d_knorm * k_scale
    d_keys = k_rate * (k_back - k_unit * jnp.mean(k_back * k_unit, axis=-1, keepdims=True))
    d_joined = jnp.concatenate([d_query, d_keys, d_values], axis=-1).astype(jnp.bfloat16)
    in_order = lax.dynamic_slice(
        jnp.concatenate([d_joined, d_joined], axis=0), (tokens - me * rows, 0), d_joined.shape
    )
    term = contract(in_order, proj_full, 1, 1).astype(jnp.bfloat16)
    d_normed = lax.psum_scatter(term, "tensor", scatter_dimension=0, tiled=True).astype(jnp.float32)
    d_proj = contract(normed, d_joined, 0, 0).astype(jnp.bfloat16)
    sent = jnp.concatenate(
        [d_proj.reshape(dp, share, three), fold_wide(d_outw.astype(jnp.bfloat16), dp, three)], axis=1
    )
    terms = lax.all_to_all(sent, "dp", 0, 0)
    total = jnp.sum(terms.astype(jnp.float32), axis=0).astype(jnp.bfloat16)
    sums = lax.all_to_all(jnp.broadcast_to(total[None], terms.shape), "dp", 0, 0)
    grad_qkv = sums[:, :share].reshape(dp * share, three)
    grad_wout = unfold_wide(sums[:, share:], w_out.shape[3])
    d_tokens = cot_rows.astype(jnp.float32) + scaled * (
        d_normed
        - jnp.mean(d_normed, axis=-1, keepdims=True)
        - unit * jnp.mean(d_normed * unit, axis=-1, keepdims=True)
    )
    passed = shifted(d_tokens.astype(jnp.bfloat16), "pipe", -1)
    return passed[None, None], grad_qkv[None, :, None, :], grad_wout[None, None]


def solution(mesh):
    placed = (
        P("dp", "pipe", "tensor", None),
        P("dp", "pipe", "tensor", None),
        P("dp", "pipe", None),
        P("pipe", "dp", "tensor", None),
        P("pipe", "tensor", "dp", None),
        P("pipe", None),
        P("pipe", None),
    )
    return jax.shard_map(
        per_device,
        mesh=mesh,
        in_specs=placed,
        out_specs=(
            P("dp", "pipe", "tensor", None),
            P("pipe", None, "tensor", None),
            P("pipe", "tensor", None, None),
        ),
        check_vma=False,
    )
```

```python
import jax
import jax.numpy as jnp
from jax import lax
from jax.experimental import pallas as pl
from jax.experimental.pallas import tpu as pltpu
from jax.sharding import PartitionSpec as P

EPS = 1e-06
BLOCK = 256
TOP = 30000.0
LEAST = 1e-30


def shifted(array, axis, by):
    peers = lax.axis_size(axis)
    return lax.ppermute(array, axis, [(i, (i + by) % peers) for i in range(peers)])


def contract(left, right, left_dim, right_dim):
    return lax.dot_general(
        left, right, (((left_dim,), (right_dim,)), ((), ())), preferred_element_type=jnp.float32
    )


def fold_wide(wide, parts, width):
    rows, cols = wide.shape
    cut = [wide[:, c : c + width].reshape(parts, rows // parts, width) for c in range(0, cols, width)]
    return jnp.concatenate(cut, axis=1)


def unfold_wide(folded, cols):
    parts, rows, width = folded.shape
    high = rows * width // cols
    cut = [folded[:, i * high : (i + 1) * high].reshape(parts * high, width) for i in range(cols // width)]
    return jnp.concatenate(cut, axis=1)


def head_kernel(
    normed, cot, proj, outw, seg_col, seg_row, q_gain, k_gain,
    term, d_joined, attended,
    q_unit, k_unit, q_rate, k_rate, q_norm, k_norm, v_low, d_att, d_key, d_val,
):
    tokens, width = q_norm.shape
    factor = width ** (-0.5)
    count = tokens // BLOCK
    for i in range(count):
        rows = pl.ds(i * BLOCK, BLOCK)
        joined = jnp.dot(normed[rows, :], proj[...], preferred_element_type=jnp.float32)
        for at, unit, rate, norm, gain in (
            (0, q_unit, q_rate, q_norm, q_gain),
            (1, k_unit, k_rate, k_norm, k_gain),
        ):
            part = joined[:, at * width : (at + 1) * width]
            r = lax.rsqrt(jnp.mean(part * part, axis=-1, keepdims=True) + EPS)
            u = part * r
            rate[rows, :] = r
            unit[rows, :] = u
            norm[rows, :] = (u * gain[...]).astype(jnp.bfloat16)
        v_low[rows, :] = joined[:, 2 * width :].astype(jnp.bfloat16)
        d_att[rows, :] = contract(cot[rows, :], outw[...], 1, 1).astype(jnp.bfloat16)
    d_key[...] = jnp.zeros_like(d_key)
    d_val[...] = jnp.zeros_like(d_val)
    for i in range(count):
        rows = pl.ds(i * BLOCK, BLOCK)
        low, high = max(i - 1, 0), min(i + 2, count)
        near = pl.ds(low * BLOCK, (high - low) * BLOCK)
        qn, kn, vb, do = q_norm[rows, :], k_norm[near, :], v_low[near, :], d_att[rows, :]
        scores = contract(qn, kn, 1, 1) * factor
        same = seg_col[rows, :] == seg_row[:, low * BLOCK : high * BLOCK]
        expd = jnp.where(same, jnp.exp(scores), 0.0)
        probs = expd / jnp.sum(expd, axis=-1, keepdims=True)
        probs_low = probs.astype(jnp.bfloat16)
        attended[rows, :] = jnp.dot(probs_low, vb, preferred_element_type=jnp.float32).astype(jnp.bfloat16)
        d_probs = contract(do, vb, 1, 1)
        d_val[near, :] += contract(probs_low, do, 0, 0)
        delta = jnp.sum(probs * d_probs, axis=-1, keepdims=True)
        d_scores = (probs * (d_probs - delta) * factor).astype(jnp.bfloat16)
        d_key[near, :] += contract(d_scores, qn, 0, 0)
        back = jnp.dot(d_scores, kn, preferred_element_type=jnp.float32) * q_gain[...]
        u = q_unit[rows, :]
        d_query = q_rate[rows, :] * (back - u * jnp.mean(back * u, axis=-1, keepdims=True))
        d_joined[rows, 0:width] = d_query.astype(jnp.bfloat16)
    for i in range(count):
        rows = pl.ds(i * BLOCK, BLOCK)
        back = d_key[rows, :] * k_gain[...]
        u = k_unit[rows, :]
        d_keys = k_rate[rows, :] * (back - u * jnp.mean(back * u, axis=-1, keepdims=True))
        d_joined[rows, width : 2 * width] = d_keys.astype(jnp.bfloat16)
        d_joined[rows, 2 * width :] = d_val[rows, :].astype(jnp.bfloat16)
        term[rows, :] = contract(d_joined[rows, :], proj[...], 1, 1).astype(jnp.bfloat16)


def head_backward(normed, cotangent, proj, outw, segments, q_scale, k_scale):
    tokens, features = normed.shape
    width = outw.shape[0]
    here = pl.BlockSpec(memory_space=pltpu.VMEM)

    def kept(columns, dtype):
        return pltpu.VMEM((tokens, columns), dtype)

    return pl.pallas_call(
        head_kernel,
        out_shape=(
            jax.ShapeDtypeStruct((tokens, features), jnp.bfloat16),
            jax.ShapeDtypeStruct((tokens, 3 * width), jnp.bfloat16),
            jax.ShapeDtypeStruct((tokens, width), jnp.bfloat16),
        ),
        in_specs=[here] * 8,
        out_specs=(here,) * 3,
        scratch_shapes=[
            kept(width, jnp.float32), kept(width, jnp.float32), kept(1, jnp.float32), kept(1, jnp.float32),
            kept(width, jnp.bfloat16), kept(width, jnp.bfloat16), kept(width, jnp.bfloat16), kept(width, jnp.bfloat16),
            kept(width, jnp.float32), kept(width, jnp.float32),
        ],
        compiler_params=pltpu.CompilerParams(vmem_limit_bytes=40 * 1024 * 1024),
        cost_estimate=pl.CostEstimate(flops=5_000_000_000, bytes_accessed=12_000_000, transcendentals=1_000_000),
    )(
        normed, cotangent, proj, outw, segments[:, None], segments[None, :], q_scale[None, :], k_scale[None, :]
    )


def per_device(saved_input, grad_in, segment_ids, w_qkv, w_out, q_gain, k_gain):
    dp = lax.axis_size("dp")
    me = lax.axis_index("tensor")
    x_float = saved_input[0, 0].astype(jnp.float32)
    rows = x_float.shape[0]
    centred = x_float - jnp.mean(x_float, axis=-1, keepdims=True)
    scaled = lax.rsqrt(jnp.mean(centred * centred, axis=-1, keepdims=True) + EPS)
    unit = centred * scaled
    cot_rows = grad_in[0, 0]
    three = w_qkv.shape[3]
    share = w_qkv.shape[1]
    weights = jnp.concatenate([w_qkv[0, :, 0, :], fold_wide(w_out[0, 0], 1, three)[0]], axis=0)
    weights = lax.all_gather(weights, "dp", axis=0)
    proj_full = weights[:, :share].reshape(dp * share, three)
    outw_full = unfold_wide(weights[:, share:], w_out.shape[3])
    low_rows = unit.astype(jnp.bfloat16)
    scales = [TOP / jnp.maximum(jnp.max(jnp.abs(b.astype(jnp.float32))), LEAST) for b in (low_rows, cot_rows)]
    sent = [(b.astype(jnp.float32) * s).astype(jnp.float16) for b, s in zip((low_rows, cot_rows), scales)]
    blocks = lax.all_gather(jnp.concatenate(sent, axis=0), "tensor", axis=0)
    peers = blocks.shape[0]
    table = jnp.zeros((peers * 16, 128), jnp.float32)
    mine = jnp.where(lax.broadcasted_iota(jnp.int32, (16, 128), 1) < 64, scales[0], scales[1])
    table = lax.psum(lax.dynamic_update_slice(table, mine, (me * 16, 0)), "tensor")
    inverse = 1.0 / table.reshape(peers, 16, 128)[:, :1, :]
    normed = (blocks[:, :rows].astype(jnp.float32) * inverse[:, :, :1]).astype(jnp.bfloat16)
    cotangent = (blocks[:, rows:].astype(jnp.float32) * inverse[:, :, 64:65]).astype(jnp.bfloat16)
    normed = normed.reshape(peers * rows, normed.shape[-1])
    cotangent = cotangent.reshape(peers * rows, cotangent.shape[-1])
    term, d_joined, attended = head_backward(
        normed, cotangent, proj_full, outw_full, segment_ids[0, 0], q_gain[0], k_gain[0]
    )
    d_outw = contract(attended, cotangent, 0, 0)
    d_normed = lax.psum_scatter(term, "tensor", scatter_dimension=0, tiled=True).astype(jnp.float32)
    d_proj = contract(normed, d_joined, 0, 0).astype(jnp.bfloat16)
    gradients = jnp.concatenate(
        [d_proj.reshape(dp, share, three), fold_wide(d_outw.astype(jnp.bfloat16), dp, three)], axis=1
    )
    terms = lax.all_to_all(gradients, "dp", 0, 0)
    total = jnp.sum(terms.astype(jnp.float32), axis=0).astype(jnp.bfloat16)
    sums = lax.all_to_all(jnp.broadcast_to(total[None], terms.shape), "dp", 0, 0)
    grad_qkv = sums[:, :share].reshape(dp * share, three)
    grad_wout = unfold_wide(sums[:, share:], w_out.shape[3])
    d_tokens = cot_rows.astype(jnp.float32) + scaled * (
        d_normed
        - jnp.mean(d_normed, axis=-1, keepdims=True)
        - unit * jnp.mean(d_normed * unit, axis=-1, keepdims=True)
    )
    passed = shifted(d_tokens.astype(jnp.bfloat16), "pipe", -1)
    return passed[None, None], grad_qkv[None, :, None, :], grad_wout[None, None]


def solution(mesh):
    placed = (
        P("dp", "pipe", "tensor", None),
        P("dp", "pipe", "tensor", None),
        P("dp", "pipe", None),
        P("pipe", "dp", "tensor", None),
        P("pipe", "tensor", "dp", None),
        P("pipe", None),
        P("pipe", None),
    )
    return jax.shard_map(
        per_device,
        mesh=mesh,
        in_specs=placed,
        out_specs=(
            P("dp", "pipe", "tensor", None),
            P("pipe", None, "tensor", None),
            P("pipe", "tensor", None, None),
        ),
        check_vma=False,
    )
```

```python
import functools

import jax
import jax.numpy as jnp
from jax import lax
from jax.experimental import pallas as pl
from jax.experimental.pallas import tpu as pltpu
from jax.sharding import PartitionSpec as P

EPS = 1e-06
BLOCK = 256


def shifted(array, axis, by):
    peers = lax.axis_size(axis)
    return lax.ppermute(array, axis, [(i, (i + by) % peers) for i in range(peers)])


def contract(left, right, left_dim, right_dim):
    return lax.dot_general(
        left, right, (((left_dim,), (right_dim,)), ((), ())), preferred_element_type=jnp.float32
    )


def ring_gather(block, axis):
    peers = lax.axis_size(axis)
    got = {0: block}
    up = down = block
    for step in range(1, peers // 2 + 1):
        up = shifted(up, axis, 1)
        got[peers - step] = up
        if step < peers - step:
            down = shifted(down, axis, -1)
            got[step] = down
    return [got[i] for i in range(peers)]


def fold_wide(wide, parts, width):
    rows, cols = wide.shape
    cut = [wide[:, c : c + width].reshape(parts, rows // parts, width) for c in range(0, cols, width)]
    return jnp.concatenate(cut, axis=1)


def unfold_wide(folded, cols):
    parts, rows, width = folded.shape
    high = rows * width // cols
    cut = [folded[:, i * high : (i + 1) * high].reshape(parts * high, width) for i in range(cols // width)]
    return jnp.concatenate(cut, axis=1)


def normalised(rows):
    x = rows.astype(jnp.float32)
    centred = x - jnp.mean(x, axis=-1, keepdims=True)
    rate = lax.rsqrt(jnp.mean(centred * centred, axis=-1, keepdims=True) + EPS)
    return centred * rate, rate


def first_kernel(tokens, cot, block):
    rows = tokens.shape[0]
    block[0:rows, :] = normalised(tokens[...])[0].astype(jnp.bfloat16)
    block[rows:, :] = cot[...]


def last_kernel(tokens, cot, d_normed, out):
    unit, rate = normalised(tokens[...])
    d = d_normed[...].astype(jnp.float32)
    inner = d - jnp.mean(d, axis=-1, keepdims=True) - unit * jnp.mean(d * unit, axis=-1, keepdims=True)
    out[...] = (cot[...].astype(jnp.float32) + rate * inner).astype(jnp.bfloat16)


def head_kernel(peers, where, weights, seg_col, seg_row, q_gain, k_gain, *rest):
    blocks, rest = rest[:peers], rest[peers:]
    term, d_joined, attended, normed, cot = rest[:5]
    (proj, outw, made, sems,
     q_unit, k_unit, q_rate, k_rate, q_norm, k_norm, v_low, d_att, d_key, d_val) = rest[5:]
    tokens, width = q_norm.shape
    share = proj.shape[0] // weights.shape[0]
    three = proj.shape[1]
    piece = width // weights.shape[0]
    for p in range(weights.shape[0]):
        proj[p * share : (p + 1) * share, :] = weights[p, 0:share, :]
        for c in range(outw.shape[1] // three):
            low = share + c * piece
            outw[p * piece : (p + 1) * piece, c * three : (c + 1) * three] = weights[p, low : low + piece, :]
    each = tokens // peers
    for d in range(peers):
        at = lax.rem(where[0, 0] + d, peers) * each
        at = pl.multiple_of(at, each)
        normed[pl.ds(at, each), :] = blocks[d][0:each, :]
        cot[pl.ds(at, each), :] = blocks[d][each:, :]
    factor = width ** (-0.5)
    count = tokens // BLOCK
    for i in range(count):
        rows = pl.ds(i * BLOCK, BLOCK)
        joined = jnp.dot(normed[rows, :], proj[...], preferred_element_type=jnp.float32)
        for at, unit, rate, norm, gain in (
            (0, q_unit, q_rate, q_norm, q_gain),
            (1, k_unit, k_rate, k_norm, k_gain),
        ):
            part = joined[:, at * width : (at + 1) * width]
            r = lax.rsqrt(jnp.mean(part * part, axis=-1, keepdims=True) + EPS)
            u = part * r
            rate[rows, :] = r
            unit[rows, :] = u
            norm[rows, :] = (u * gain[...]).astype(jnp.bfloat16)
        v_low[rows, :] = joined[:, 2 * width :].astype(jnp.bfloat16)
        d_att[rows, :] = contract(cot[rows, :], outw[...], 1, 1).astype(jnp.bfloat16)
    d_key[...] = jnp.zeros_like(d_key)
    d_val[...] = jnp.zeros_like(d_val)
    copies = []
    for i in range(count + 1):
        if i < count:
            rows = pl.ds(i * BLOCK, BLOCK)
            low, high = max(i - 1, 0), min(i + 2, count)
            near = pl.ds(low * BLOCK, (high - low) * BLOCK)
            qn, kn, vb, do = q_norm[rows, :], k_norm[near, :], v_low[near, :], d_att[rows, :]
            scores = contract(qn, kn, 1, 1) * factor
            same = seg_col[rows, :] == seg_row[:, low * BLOCK : high * BLOCK]
            expd = jnp.where(same, jnp.exp(scores), 0.0)
            probs = expd / jnp.sum(expd, axis=-1, keepdims=True)
            probs_low = probs.astype(jnp.bfloat16)
            attended[rows, :] = jnp.dot(probs_low, vb, preferred_element_type=jnp.float32).astype(jnp.bfloat16)
            d_probs = contract(do, vb, 1, 1)
            d_val[near, :] += contract(probs_low, do, 0, 0)
            delta = jnp.sum(probs * d_probs, axis=-1, keepdims=True)
            d_scores = (probs * (d_probs - delta) * factor).astype(jnp.bfloat16)
            d_key[near, :] += contract(d_scores, qn, 0, 0)
            back = jnp.dot(d_scores, kn, preferred_element_type=jnp.float32) * q_gain[...]
            u = q_unit[rows, :]
            d_query = q_rate[rows, :] * (back - u * jnp.mean(back * u, axis=-1, keepdims=True))
            d_joined[rows, 0:width] = d_query.astype(jnp.bfloat16)
        if i > 0:
            rows = pl.ds((i - 1) * BLOCK, BLOCK)
            back = d_key[rows, :] * k_gain[...]
            u = k_unit[rows, :]
            d_keys = k_rate[rows, :] * (back - u * jnp.mean(back * u, axis=-1, keepdims=True))
            d_joined[rows, width : 2 * width] = d_keys.astype(jnp.bfloat16)
            d_joined[rows, 2 * width :] = d_val[rows, :].astype(jnp.bfloat16)
            made[rows, :] = contract(d_joined[rows, :], proj[...], 1, 1).astype(jnp.bfloat16)
            copy = pltpu.make_async_copy(made.at[rows, :], term.at[rows, :], sems.at[i - 1])
            copy.start()
            copies.append(copy)
    for copy in copies:
        copy.wait()


def head_backward(blocks, weights, share, segments, q_scale, k_scale, me):
    peers = len(blocks)
    tokens = segments.shape[0]
    features = blocks[0].shape[1]
    width = q_scale.shape[0]
    here = pl.BlockSpec(memory_space=pltpu.VMEM)
    low = jnp.bfloat16

    def kept(columns, dtype):
        return pltpu.VMEM((tokens, columns), dtype)

    return pl.pallas_call(
        functools.partial(head_kernel, peers),
        out_shape=tuple(
            jax.ShapeDtypeStruct((tokens, columns), low) for columns in (features, 3 * width, width, features, features)
        ),
        in_specs=[pl.BlockSpec(memory_space=pltpu.SMEM)] + [here] * (5 + peers),
        out_specs=(pl.BlockSpec(memory_space=pl.ANY),) + (here,) * 4,
        scratch_shapes=[
            pltpu.VMEM((features, 3 * width), low), pltpu.VMEM((width, features), low), kept(features, low),
            pltpu.SemaphoreType.DMA((tokens // BLOCK,)),
            kept(width, jnp.float32), kept(width, jnp.float32), kept(1, jnp.float32), kept(1, jnp.float32),
            kept(width, low), kept(width, low), kept(width, low), kept(width, low),
            kept(width, jnp.float32), kept(width, jnp.float32),
        ],
        compiler_params=pltpu.CompilerParams(vmem_limit_bytes=48 * 1024 * 1024),
        cost_estimate=pl.CostEstimate(flops=5_000_000_000, bytes_accessed=12_000_000, transcendentals=1_000_000),
    )(
        me.reshape(1, 1), weights, segments[:, None], segments[None, :], q_scale[None, :], k_scale[None, :], *blocks
    )


def per_device(saved_input, grad_in, segment_ids, w_qkv, w_out, q_gain, k_gain):
    dp = lax.axis_size("dp")
    me = lax.axis_index("tensor").astype(jnp.int32)
    tokens, cot = saved_input[0, 0], grad_in[0, 0]
    three = w_qkv.shape[3]
    share = w_qkv.shape[1]
    here = pl.BlockSpec(memory_space=pltpu.VMEM)
    weights = jnp.concatenate([w_qkv[0, :, 0, :], fold_wide(w_out[0, 0], 1, three)[0]], axis=0)
    weights = lax.all_gather(weights, "dp", axis=0)
    block = pl.pallas_call(
        first_kernel,
        out_shape=jax.ShapeDtypeStruct((2 * tokens.shape[0], tokens.shape[1]), jnp.bfloat16),
        in_specs=[here, here],
        out_specs=here,
    )(tokens, cot)
    blocks = ring_gather(block, "tensor")
    term, d_joined, attended, normed, cotangent = head_backward(
        blocks, weights, share, segment_ids[0, 0], q_gain[0], k_gain[0], me
    )
    d_normed = lax.psum_scatter(term, "tensor", scatter_dimension=0, tiled=True)
    d_outw = contract(attended, cotangent, 0, 0)
    d_proj = contract(normed, d_joined, 0, 0).astype(jnp.bfloat16)
    gradients = jnp.concatenate(
        [d_proj.reshape(dp, share, three), fold_wide(d_outw.astype(jnp.bfloat16), dp, three)], axis=1
    )
    terms = lax.all_to_all(gradients, "dp", 0, 0)
    total = jnp.sum(terms.astype(jnp.float32), axis=0).astype(jnp.bfloat16)
    sums = lax.all_to_all(jnp.broadcast_to(total[None], terms.shape), "dp", 0, 0)
    grad_qkv = sums[:, :share].reshape(dp * share, three)
    grad_wout = unfold_wide(sums[:, share:], w_out.shape[3])
    d_tokens = pl.pallas_call(
        last_kernel,
        out_shape=jax.ShapeDtypeStruct(tokens.shape, jnp.bfloat16),
        in_specs=[here] * 3,
        out_specs=here,
    )(tokens, cot, d_normed)
    passed = shifted(d_tokens, "pipe", -1)
    return passed[None, None], grad_qkv[None, :, None, :], grad_wout[None, None]


def solution(mesh):
    placed = (
        P("dp", "pipe", "tensor", None),
        P("dp", "pipe", "tensor", None),
        P("dp", "pipe", None),
        P("pipe", "dp", "tensor", None),
        P("pipe", "tensor", "dp", None),
        P("pipe", None),
        P("pipe", None),
    )
    return jax.shard_map(
        per_device,
        mesh=mesh,
        in_specs=placed,
        out_specs=(
            P("dp", "pipe", "tensor", None),
            P("pipe", None, "tensor", None),
            P("pipe", "tensor", None, None),
        ),
        check_vma=False,
    )
```

```python
import jax
import jax.numpy as jnp
from jax import lax
from jax.experimental import pallas as pl
from jax.experimental.pallas import tpu as pltpu
from jax.sharding import PartitionSpec as P

EPS = 1e-06
BLOCK = 256
TOP = 30000.0
LEAST = 1e-30
NOTE = 8


def shifted(array, axis, by):
    peers = lax.axis_size(axis)
    return lax.ppermute(array, axis, [(i, (i + by) % peers) for i in range(peers)])


def contract(left, right, left_dim, right_dim):
    return lax.dot_general(
        left, right, (((left_dim,), (right_dim,)), ((), ())), preferred_element_type=jnp.float32
    )


def fold_wide(wide, parts, width):
    rows, cols = wide.shape
    cut = [wide[:, c : c + width].reshape(parts, rows // parts, width) for c in range(0, cols, width)]
    return jnp.concatenate(cut, axis=1)


def unfold_wide(folded, cols):
    parts, rows, width = folded.shape
    high = rows * width // cols
    cut = [folded[:, i * high : (i + 1) * high].reshape(parts * high, width) for i in range(cols // width)]
    return jnp.concatenate(cut, axis=1)


def normalised(rows):
    x = rows.astype(jnp.float32)
    centred = x - jnp.mean(x, axis=-1, keepdims=True)
    rate = lax.rsqrt(jnp.mean(centred * centred, axis=-1, keepdims=True) + EPS)
    return centred * rate, rate


def first_kernel(tokens, cot, w_in, w_out, block, weights):
    rows, columns = tokens.shape
    share, three = w_in.shape
    weights[0:share, :] = w_in[...]
    for c in range(columns // three):
        low = share + c * w_out.shape[0]
        weights[low : low + w_out.shape[0], :] = w_out[:, c * three : (c + 1) * three]
    halves = (normalised(tokens[...])[0].astype(jnp.bfloat16).astype(jnp.float32), cot[...].astype(jnp.float32))
    for at, half in enumerate(halves):
        most = jnp.max(jnp.max(jnp.abs(half), axis=1, keepdims=True), axis=0, keepdims=True)
        power = jnp.floor(jnp.log2(TOP / jnp.maximum(most, LEAST)))
        block[at * rows : (at + 1) * rows, :] = half * jnp.exp2(power)
        wide = columns // 2
        block[2 * rows :, at * wide : (at + 1) * wide] = jnp.broadcast_to(power, (NOTE, wide))


def last_kernel(tokens, cot, d_normed, out):
    unit, rate = normalised(tokens[...])
    d = d_normed[...].astype(jnp.float32)
    inner = d - jnp.mean(d, axis=-1, keepdims=True) - unit * jnp.mean(d * unit, axis=-1, keepdims=True)
    out[...] = (cot[...].astype(jnp.float32) + rate * inner).astype(jnp.bfloat16)


def head_kernel(
    normed, cot, weights, seg_col, seg_row, q_gain, k_gain,
    term, d_joined, attended,
    proj, outw, made, sems,
    q_unit, k_unit, q_rate, k_rate, q_norm, k_norm, v_low, d_att, d_key, d_val,
):
    tokens, width = q_norm.shape
    share = proj.shape[0] // weights.shape[0]
    three = proj.shape[1]
    piece = width // weights.shape[0]
    for p in range(weights.shape[0]):
        proj[p * share : (p + 1) * share, :] = weights[p, 0:share, :]
        for c in range(outw.shape[1] // three):
            low = share + c * piece
            outw[p * piece : (p + 1) * piece, c * three : (c + 1) * three] = weights[p, low : low + piece, :]
    factor = width ** (-0.5)
    count = tokens // BLOCK
    for i in range(count):
        rows = pl.ds(i * BLOCK, BLOCK)
        joined = jnp.dot(normed[rows, :], proj[...], preferred_element_type=jnp.float32)
        for at, unit, rate, norm, gain in (
            (0, q_unit, q_rate, q_norm, q_gain),
            (1, k_unit, k_rate, k_norm, k_gain),
        ):
            part = joined[:, at * width : (at + 1) * width]
            r = lax.rsqrt(jnp.mean(part * part, axis=-1, keepdims=True) + EPS)
            u = part * r
            rate[rows, :] = r
            unit[rows, :] = u
            norm[rows, :] = (u * gain[...]).astype(jnp.bfloat16)
        v_low[rows, :] = joined[:, 2 * width :].astype(jnp.bfloat16)
        d_att[rows, :] = contract(cot[rows, :], outw[...], 1, 1).astype(jnp.bfloat16)
    d_key[...] = jnp.zeros_like(d_key)
    d_val[...] = jnp.zeros_like(d_val)
    copies = []
    for i in range(count + 1):
        if i < count:
            rows = pl.ds(i * BLOCK, BLOCK)
            low, high = max(i - 1, 0), min(i + 2, count)
            near = pl.ds(low * BLOCK, (high - low) * BLOCK)
            qn, kn, vb, do = q_norm[rows, :], k_norm[near, :], v_low[near, :], d_att[rows, :]
            scores = contract(qn, kn, 1, 1) * factor
            same = seg_col[rows, :] == seg_row[:, low * BLOCK : high * BLOCK]
            expd = jnp.where(same, jnp.exp(scores), 0.0)
            probs = expd / jnp.sum(expd, axis=-1, keepdims=True)
            probs_low = probs.astype(jnp.bfloat16)
            attended[rows, :] = jnp.dot(probs_low, vb, preferred_element_type=jnp.float32).astype(jnp.bfloat16)
            d_probs = contract(do, vb, 1, 1)
            d_val[near, :] += contract(probs_low, do, 0, 0)
            delta = jnp.sum(probs * d_probs, axis=-1, keepdims=True)
            d_scores = (probs * (d_probs - delta) * factor).astype(jnp.bfloat16)
            d_key[near, :] += contract(d_scores, qn, 0, 0)
            back = jnp.dot(d_scores, kn, preferred_element_type=jnp.float32) * q_gain[...]
            u = q_unit[rows, :]
            d_query = q_rate[rows, :] * (back - u * jnp.mean(back * u, axis=-1, keepdims=True))
            d_joined[rows, 0:width] = d_query.astype(jnp.bfloat16)
        if i > 0:
            rows = pl.ds((i - 1) * BLOCK, BLOCK)
            back = d_key[rows, :] * k_gain[...]
            u = k_unit[rows, :]
            d_keys = k_rate[rows, :] * (back - u * jnp.mean(back * u, axis=-1, keepdims=True))
            d_joined[rows, width : 2 * width] = d_keys.astype(jnp.bfloat16)
            d_joined[rows, 2 * width :] = d_val[rows, :].astype(jnp.bfloat16)
            made[rows, :] = contract(d_joined[rows, :], proj[...], 1, 1).astype(jnp.bfloat16)
            copy = pltpu.make_async_copy(made.at[rows, :], term.at[rows, :], sems.at[i - 1])
            copy.start()
            copies.append(copy)
    for copy in copies:
        copy.wait()


def head_backward(normed, cotangent, weights, segments, q_scale, k_scale):
    tokens, features = normed.shape
    width = q_scale.shape[0]
    here = pl.BlockSpec(memory_space=pltpu.VMEM)
    low = jnp.bfloat16

    def kept(columns, dtype):
        return pltpu.VMEM((tokens, columns), dtype)

    return pl.pallas_call(
        head_kernel,
        out_shape=tuple(
            jax.ShapeDtypeStruct((tokens, columns), low) for columns in (features, 3 * width, width)
        ),
        in_specs=[here] * 7,
        out_specs=(pl.BlockSpec(memory_space=pl.ANY), here, here),
        scratch_shapes=[
            pltpu.VMEM((features, 3 * width), low), pltpu.VMEM((width, features), low), kept(features, low),
            pltpu.SemaphoreType.DMA((tokens // BLOCK,)),
            kept(width, jnp.float32), kept(width, jnp.float32), kept(1, jnp.float32), kept(1, jnp.float32),
            kept(width, low), kept(width, low), kept(width, low), kept(width, low),
            kept(width, jnp.float32), kept(width, jnp.float32),
        ],
        compiler_params=pltpu.CompilerParams(vmem_limit_bytes=48 * 1024 * 1024),
        cost_estimate=pl.CostEstimate(flops=5_000_000_000, bytes_accessed=12_000_000, transcendentals=1_000_000),
    )(
        normed, cotangent, weights, segments[:, None], segments[None, :], q_scale[None, :], k_scale[None, :]
    )


def per_device(saved_input, grad_in, segment_ids, w_qkv, w_out, q_gain, k_gain):
    dp = lax.axis_size("dp")
    tokens, cot = saved_input[0, 0], grad_in[0, 0]
    three = w_qkv.shape[3]
    share = w_qkv.shape[1]
    here = pl.BlockSpec(memory_space=pltpu.VMEM)
    rows, features = tokens.shape
    block, weights = pl.pallas_call(
        first_kernel,
        out_shape=(
            jax.ShapeDtypeStruct((2 * rows + NOTE, features), jnp.float32),
            jax.ShapeDtypeStruct((share + w_out.shape[2] * features // three, three), jnp.bfloat16),
        ),
        in_specs=[here] * 4,
        out_specs=(here, here),
    )(tokens, cot, w_qkv[0, :, 0, :], w_out[0, 0])
    weights = lax.all_gather(weights, "dp", axis=0)
    blocks = lax.all_gather(block.astype(jnp.float16), "tensor", axis=0)
    powers = blocks[:, 2 * rows : 2 * rows + 1, :].astype(jnp.float32)
    halves = (
        blocks[:, at * rows : (at + 1) * rows].astype(jnp.float32)
        * jnp.exp2(-powers[:, :, at * features // 2 : at * features // 2 + 1])
        for at in (0, 1)
    )
    normed, cotangent = (half.astype(jnp.bfloat16).reshape(-1, features) for half in halves)
    term, d_joined, attended = head_backward(
        normed, cotangent, weights, segment_ids[0, 0], q_gain[0], k_gain[0]
    )
    d_normed = lax.psum_scatter(term, "tensor", scatter_dimension=0, tiled=True)
    d_outw = contract(attended, cotangent, 0, 0)
    d_proj = contract(normed, d_joined, 0, 0).astype(jnp.bfloat16)
    gradients = jnp.concatenate(
        [d_proj.reshape(dp, share, three), fold_wide(d_outw.astype(jnp.bfloat16), dp, three)], axis=1
    )
    terms = lax.all_to_all(gradients, "dp", 0, 0)
    total = jnp.sum(terms.astype(jnp.float32), axis=0).astype(jnp.bfloat16)
    sums = lax.all_to_all(jnp.broadcast_to(total[None], terms.shape), "dp", 0, 0)
    grad_qkv = sums[:, :share].reshape(dp * share, three)
    grad_wout = unfold_wide(sums[:, share:], w_out.shape[3])
    d_tokens = pl.pallas_call(
        last_kernel,
        out_shape=jax.ShapeDtypeStruct(tokens.shape, jnp.bfloat16),
        in_specs=[here] * 3,
        out_specs=here,
    )(tokens, cot, d_normed)
    passed = shifted(d_tokens, "pipe", -1)
    return passed[None, None], grad_qkv[None, :, None, :], grad_wout[None, None]


def solution(mesh):
    placed = (
        P("dp", "pipe", "tensor", None),
        P("dp", "pipe", "tensor", None),
        P("dp", "pipe", None),
        P("pipe", "dp", "tensor", None),
        P("pipe", "tensor", "dp", None),
        P("pipe", None),
        P("pipe", None),
    )
    return jax.shard_map(
        per_device,
        mesh=mesh,
        in_specs=placed,
        out_specs=(
            P("dp", "pipe", "tensor", None),
            P("pipe", None, "tensor", None),
            P("pipe", "tensor", None, None),
        ),
        check_vma=False,
    )
```

```python
import jax
import jax.numpy as jnp
from jax import lax
from jax.experimental import pallas as pl
from jax.experimental.pallas import tpu as pltpu
from jax.sharding import PartitionSpec as P

EPS = 1e-06
BLOCK = 256
TOP = 30000.0
LEAST = 1e-30
NOTE = 8


def shifted(array, axis, by):
    peers = lax.axis_size(axis)
    return lax.ppermute(array, axis, [(i, (i + by) % peers) for i in range(peers)])


def contract(left, right, left_dim, right_dim):
    return lax.dot_general(
        left, right, (((left_dim,), (right_dim,)), ((), ())), preferred_element_type=jnp.float32
    )


def fold_wide(wide, parts, width):
    rows, cols = wide.shape
    cut = [wide[:, c : c + width].reshape(parts, rows // parts, width) for c in range(0, cols, width)]
    return jnp.concatenate(cut, axis=1)


def unfold_wide(folded, cols):
    parts, rows, width = folded.shape
    high = rows * width // cols
    cut = [folded[:, i * high : (i + 1) * high].reshape(parts * high, width) for i in range(cols // width)]
    return jnp.concatenate(cut, axis=1)


def normalised(rows):
    x = rows.astype(jnp.float32)
    centred = x - jnp.mean(x, axis=-1, keepdims=True)
    rate = lax.rsqrt(jnp.mean(centred * centred, axis=-1, keepdims=True) + EPS)
    return centred * rate, rate


def first_kernel(tokens, cot, w_in, w_out, block, weights):
    rows, columns = tokens.shape
    share, three = w_in.shape
    weights[0:share, :] = w_in[...]
    for c in range(columns // three):
        low = share + c * w_out.shape[0]
        weights[low : low + w_out.shape[0], :] = w_out[:, c * three : (c + 1) * three]
    halves = (normalised(tokens[...])[0].astype(jnp.bfloat16).astype(jnp.float32), cot[...].astype(jnp.float32))
    for at, half in enumerate(halves):
        most = jnp.max(jnp.max(jnp.abs(half), axis=1, keepdims=True), axis=0, keepdims=True)
        power = jnp.floor(jnp.log2(TOP / jnp.maximum(most, LEAST)))
        block[at * rows : (at + 1) * rows, :] = half * jnp.exp2(power)
        wide = columns // 2
        block[2 * rows :, at * wide : (at + 1) * wide] = jnp.broadcast_to(power, (NOTE, wide))


def last_kernel(tokens, cot, d_normed, out):
    unit, rate = normalised(tokens[...])
    d = d_normed[...].astype(jnp.float32)
    inner = d - jnp.mean(d, axis=-1, keepdims=True) - unit * jnp.mean(d * unit, axis=-1, keepdims=True)
    out[...] = (cot[...].astype(jnp.float32) + rate * inner).astype(jnp.bfloat16)


def head_kernel(
    normed, cot, weights, seg_col, seg_row, q_gain, k_gain,
    term, d_joined, attended,
    proj, outw, made, sems,
    q_unit, k_unit, q_rate, k_rate, q_norm, k_norm, v_low, d_att, d_key, d_val, k_turned, v_turned,
):
    tokens, width = q_norm.shape
    share = proj.shape[0] // weights.shape[0]
    three = proj.shape[1]
    piece = width // weights.shape[0]
    for p in range(weights.shape[0]):
        proj[p * share : (p + 1) * share, :] = weights[p, 0:share, :]
        for c in range(outw.shape[1] // three):
            low = share + c * piece
            outw[p * piece : (p + 1) * piece, c * three : (c + 1) * three] = weights[p, low : low + piece, :]
    factor = width ** (-0.5)
    count = tokens // BLOCK
    for i in range(count):
        rows = pl.ds(i * BLOCK, BLOCK)
        joined = jnp.dot(normed[rows, :], proj[...], preferred_element_type=jnp.float32)
        for at, unit, rate, norm, gain in (
            (0, q_unit, q_rate, q_norm, q_gain),
            (1, k_unit, k_rate, k_norm, k_gain),
        ):
            part = joined[:, at * width : (at + 1) * width]
            r = lax.rsqrt(jnp.mean(part * part, axis=-1, keepdims=True) + EPS)
            u = part * r
            rate[rows, :] = r
            unit[rows, :] = u
            norm[rows, :] = (u * gain[...]).astype(jnp.bfloat16)
        v_low[rows, :] = joined[:, 2 * width :].astype(jnp.bfloat16)
        v_turned[:, rows] = joined[:, 2 * width :].T.astype(jnp.bfloat16)
        k_turned[:, rows] = (k_unit[rows, :] * k_gain[...]).T.astype(jnp.bfloat16)
        d_att[rows, :] = contract(cot[rows, :], outw[...], 1, 1).astype(jnp.bfloat16)
    d_key[...] = jnp.zeros_like(d_key)
    d_val[...] = jnp.zeros_like(d_val)
    copies = []
    for i in range(count + 1):
        if i < count:
            rows = pl.ds(i * BLOCK, BLOCK)
            low, high = max(i - 1, 0), min(i + 2, count)
            near = pl.ds(low * BLOCK, (high - low) * BLOCK)
            qn, do = q_norm[rows, :], d_att[rows, :]
            scores = contract(k_norm[near, :], qn, 1, 1) * factor
            same = seg_col[near, :] == seg_row[:, i * BLOCK : (i + 1) * BLOCK]
            expd = jnp.where(same, jnp.exp(scores), 0.0)
            probs = expd * (1.0 / jnp.sum(expd, axis=0, keepdims=True))
            probs_low = probs.astype(jnp.bfloat16)
            attended[:, rows] = jnp.dot(
                v_turned[:, near], probs_low, preferred_element_type=jnp.float32
            ).astype(jnp.bfloat16)
            d_probs = contract(v_low[near, :], do, 1, 1)
            d_val[near, :] += jnp.dot(probs_low, do, preferred_element_type=jnp.float32)
            delta = jnp.sum(probs * d_probs, axis=0, keepdims=True)
            d_scores = (probs * (d_probs - delta) * factor).astype(jnp.bfloat16)
            d_key[near, :] += jnp.dot(d_scores, qn, preferred_element_type=jnp.float32)
            turned = jnp.dot(k_turned[:, near], d_scores, preferred_element_type=jnp.float32)
            back = turned.T * q_gain[...]
            u = q_unit[rows, :]
            d_query = q_rate[rows, :] * (back - u * jnp.mean(back * u, axis=-1, keepdims=True))
            d_joined[rows, 0:width] = d_query.astype(jnp.bfloat16)
        if i > 0:
            rows = pl.ds((i - 1) * BLOCK, BLOCK)
            back = d_key[rows, :] * k_gain[...]
            u = k_unit[rows, :]
            d_keys = k_rate[rows, :] * (back - u * jnp.mean(back * u, axis=-1, keepdims=True))
            d_joined[rows, width : 2 * width] = d_keys.astype(jnp.bfloat16)
            d_joined[rows, 2 * width :] = d_val[rows, :].astype(jnp.bfloat16)
            made[rows, :] = contract(d_joined[rows, :], proj[...], 1, 1).astype(jnp.bfloat16)
            copy = pltpu.make_async_copy(made.at[rows, :], term.at[rows, :], sems.at[i - 1])
            copy.start()
            copies.append(copy)
    for copy in copies:
        copy.wait()


def head_backward(normed, cotangent, weights, segments, q_scale, k_scale):
    tokens, features = normed.shape
    width = q_scale.shape[0]
    here = pl.BlockSpec(memory_space=pltpu.VMEM)
    low = jnp.bfloat16

    def kept(columns, dtype):
        return pltpu.VMEM((tokens, columns), dtype)

    return pl.pallas_call(
        head_kernel,
        out_shape=tuple(
            jax.ShapeDtypeStruct(shape, low) for shape in ((tokens, features), (tokens, 3 * width), (width, tokens))
        ),
        in_specs=[here] * 7,
        out_specs=(pl.BlockSpec(memory_space=pl.ANY), here, here),
        scratch_shapes=[
            pltpu.VMEM((features, 3 * width), low), pltpu.VMEM((width, features), low), kept(features, low),
            pltpu.SemaphoreType.DMA((tokens // BLOCK,)),
            kept(width, jnp.float32), kept(width, jnp.float32), kept(1, jnp.float32), kept(1, jnp.float32),
            kept(width, low), kept(width, low), kept(width, low), kept(width, low),
            kept(width, jnp.float32), kept(width, jnp.float32),
            pltpu.VMEM((width, tokens), low), pltpu.VMEM((width, tokens), low),
        ],
        compiler_params=pltpu.CompilerParams(vmem_limit_bytes=28 * 1024 * 1024),
        cost_estimate=pl.CostEstimate(flops=5_000_000_000, bytes_accessed=12_000_000, transcendentals=1_000_000),
    )(
        normed, cotangent, weights, segments[:, None], segments[None, :], q_scale[None, :], k_scale[None, :]
    )


def per_device(saved_input, grad_in, segment_ids, w_qkv, w_out, q_gain, k_gain):
    dp = lax.axis_size("dp")
    tokens, cot = saved_input[0, 0], grad_in[0, 0]
    three = w_qkv.shape[3]
    share = w_qkv.shape[1]
    here = pl.BlockSpec(memory_space=pltpu.VMEM)
    rows, features = tokens.shape
    block, weights = pl.pallas_call(
        first_kernel,
        out_shape=(
            jax.ShapeDtypeStruct((2 * rows + NOTE, features), jnp.float32),
            jax.ShapeDtypeStruct((share + w_out.shape[2] * features // three, three), jnp.bfloat16),
        ),
        in_specs=[here] * 4,
        out_specs=(here, here),
    )(tokens, cot, w_qkv[0, :, 0, :], w_out[0, 0])
    weights = lax.all_gather(weights, "dp", axis=0)
    blocks = lax.all_gather(block.astype(jnp.float16), "tensor", axis=0)
    powers = blocks[:, 2 * rows : 2 * rows + 1, :].astype(jnp.float32)
    halves = (
        blocks[:, at * rows : (at + 1) * rows].astype(jnp.float32)
        * jnp.exp2(-powers[:, :, at * features // 2 : at * features // 2 + 1])
        for at in (0, 1)
    )
    normed, cotangent = (half.astype(jnp.bfloat16).reshape(-1, features) for half in halves)
    term, d_joined, attended = head_backward(
        normed, cotangent, weights, segment_ids[0, 0], q_gain[0], k_gain[0]
    )
    d_normed = lax.psum_scatter(term, "tensor", scatter_dimension=0, tiled=True)
    d_outw = contract(attended, cotangent, 1, 0)
    d_proj = contract(normed, d_joined, 0, 0).astype(jnp.bfloat16)
    gradients = jnp.concatenate(
        [d_proj.reshape(dp, share, three), fold_wide(d_outw.astype(jnp.bfloat16), dp, three)], axis=1
    )
    terms = lax.all_to_all(gradients, "dp", 0, 0)
    total = jnp.sum(terms.astype(jnp.float32), axis=0).astype(jnp.bfloat16)
    sums = lax.all_to_all(jnp.broadcast_to(total[None], terms.shape), "dp", 0, 0)
    grad_qkv = sums[:, :share].reshape(dp * share, three)
    grad_wout = unfold_wide(sums[:, share:], w_out.shape[3])
    d_tokens = pl.pallas_call(
        last_kernel,
        out_shape=jax.ShapeDtypeStruct(tokens.shape, jnp.bfloat16),
        in_specs=[here] * 3,
        out_specs=here,
    )(tokens, cot, d_normed)
    passed = shifted(d_tokens, "pipe", -1)
    return passed[None, None], grad_qkv[None, :, None, :], grad_wout[None, None]


def solution(mesh):
    placed = (
        P("dp", "pipe", "tensor", None),
        P("dp", "pipe", "tensor", None),
        P("dp", "pipe", None),
        P("pipe", "dp", "tensor", None),
        P("pipe", "tensor", "dp", None),
        P("pipe", None),
        P("pipe", None),
    )
    return jax.shard_map(
        per_device,
        mesh=mesh,
        in_specs=placed,
        out_specs=(
            P("dp", "pipe", "tensor", None),
            P("pipe", None, "tensor", None),
            P("pipe", "tensor", None, None),
        ),
        check_vma=False,
    )
```

```python
import jax
import jax.numpy as jnp
from jax import lax
from jax.experimental import pallas as pl
from jax.experimental.pallas import tpu as pltpu
from jax.sharding import PartitionSpec as P

EPS = 1e-06
BLOCK = 256
TOP = 30000.0
LEAST = 1e-30
NOTE = 8


def shifted(array, axis, by):
    peers = lax.axis_size(axis)
    return lax.ppermute(array, axis, [(i, (i + by) % peers) for i in range(peers)])


def contract(left, right, left_dim, right_dim):
    return lax.dot_general(
        left, right, (((left_dim,), (right_dim,)), ((), ())), preferred_element_type=jnp.float32
    )


def fold_wide(wide, parts, width):
    rows, cols = wide.shape
    cut = [wide[:, c : c + width].reshape(parts, rows // parts, width) for c in range(0, cols, width)]
    return jnp.concatenate(cut, axis=1)


def unfold_wide(folded, cols):
    parts, rows, width = folded.shape
    high = rows * width // cols
    cut = [folded[:, i * high : (i + 1) * high].reshape(parts * high, width) for i in range(cols // width)]
    return jnp.concatenate(cut, axis=1)


def normalised(rows):
    x = rows.astype(jnp.float32)
    centred = x - jnp.mean(x, axis=-1, keepdims=True)
    rate = lax.rsqrt(jnp.mean(centred * centred, axis=-1, keepdims=True) + EPS)
    return centred * rate, rate


def first_kernel(tokens, cot, w_in, w_out, block, weights):
    rows, columns = tokens.shape
    share, three = w_in.shape
    weights[0:share, :] = w_in[...]
    for c in range(columns // three):
        low = share + c * w_out.shape[0]
        weights[low : low + w_out.shape[0], :] = w_out[:, c * three : (c + 1) * three]
    halves = (normalised(tokens[...])[0].astype(jnp.bfloat16).astype(jnp.float32), cot[...].astype(jnp.float32))
    for at, half in enumerate(halves):
        most = jnp.max(jnp.max(jnp.abs(half), axis=1, keepdims=True), axis=0, keepdims=True)
        power = jnp.floor(jnp.log2(TOP / jnp.maximum(most, LEAST)))
        block[at * rows : (at + 1) * rows, :] = half * jnp.exp2(power)
        wide = columns // 2
        block[2 * rows :, at * wide : (at + 1) * wide] = jnp.broadcast_to(power, (NOTE, wide))


def last_kernel(tokens, cot, d_normed, out):
    unit, rate = normalised(tokens[...])
    d = d_normed[...].astype(jnp.float32)
    inner = d - jnp.mean(d, axis=-1, keepdims=True) - unit * jnp.mean(d * unit, axis=-1, keepdims=True)
    out[...] = (cot[...].astype(jnp.float32) + rate * inner).astype(jnp.bfloat16)


def head_kernel(
    blocks, weights, seg_col, seg_row, q_gain, k_gain,
    term, d_scaled, attended,
    proj, outw, made, d_joined, sems,
    q_unit, k_unit, q_rate, k_rate, q_norm, k_norm, v_low, d_att, d_key, d_val, k_turned, v_turned, x_scale, g_scale,
):
    tokens, width = q_norm.shape
    share = proj.shape[0] // weights.shape[0]
    three = proj.shape[1]
    piece = width // weights.shape[0]
    for p in range(weights.shape[0]):
        proj[p * share : (p + 1) * share, :] = weights[p, 0:share, :]
        for c in range(outw.shape[1] // three):
            low = share + c * piece
            outw[p * piece : (p + 1) * piece, c * three : (c + 1) * three] = weights[p, low : low + piece, :]
    factor = width ** (-0.5)
    count = tokens // BLOCK
    each = tokens // blocks.shape[0]
    features = blocks.shape[2]
    for i in range(count):
        rows = pl.ds(i * BLOCK, BLOCK)
        some = slice(i * BLOCK // each, (i + 1) * BLOCK // each)
        for at, scale in ((0, x_scale), (features // 2, g_scale)):
            power = blocks[some, 2 * each : 2 * each + 1, at : at + 1].astype(jnp.float32)
            scale[rows, :] = jnp.broadcast_to(jnp.exp2(-power), (BLOCK // each, each, 1)).reshape(BLOCK, 1)
        normed = blocks[some, 0:each, :].reshape(BLOCK, features)
        cot = blocks[some, each : 2 * each, :].reshape(BLOCK, features)
        joined = jnp.dot(normed, proj[...], preferred_element_type=jnp.float32) * x_scale[rows, :]
        for at, unit, rate, norm, gain in (
            (0, q_unit, q_rate, q_norm, q_gain),
            (1, k_unit, k_rate, k_norm, k_gain),
        ):
            part = joined[:, at * width : (at + 1) * width]
            r = lax.rsqrt(jnp.mean(part * part, axis=-1, keepdims=True) + EPS)
            u = part * r
            rate[rows, :] = r
            unit[rows, :] = u
            norm[rows, :] = (u * gain[...]).astype(jnp.bfloat16)
        v_low[rows, :] = joined[:, 2 * width :].astype(jnp.bfloat16)
        v_turned[:, rows] = joined[:, 2 * width :].T.astype(jnp.bfloat16)
        k_turned[:, rows] = (k_unit[rows, :] * k_gain[...]).T.astype(jnp.bfloat16)
        d_att[rows, :] = (contract(cot, outw[...], 1, 1) * g_scale[rows, :]).astype(jnp.bfloat16)
    d_key[...] = jnp.zeros_like(d_key)
    d_val[...] = jnp.zeros_like(d_val)
    copies = []
    for i in range(count + 1):
        if i < count:
            rows = pl.ds(i * BLOCK, BLOCK)
            low, high = max(i - 1, 0), min(i + 2, count)
            near = pl.ds(low * BLOCK, (high - low) * BLOCK)
            qn, do = q_norm[rows, :], d_att[rows, :]
            scores = contract(k_norm[near, :], qn, 1, 1) * factor
            same = seg_col[near, :] == seg_row[:, i * BLOCK : (i + 1) * BLOCK]
            expd = jnp.where(same, jnp.exp(scores), 0.0)
            probs = expd * (1.0 / jnp.sum(expd, axis=0, keepdims=True))
            probs_low = probs.astype(jnp.bfloat16)
            out = jnp.dot(v_turned[:, near], probs_low, preferred_element_type=jnp.float32).astype(jnp.bfloat16)
            across = jnp.broadcast_to(g_scale[rows, :], (BLOCK, 8)).T[0:1, :]
            attended[:, rows] = (out.astype(jnp.float32) * across).astype(jnp.bfloat16)
            d_probs = contract(v_low[near, :], do, 1, 1)
            d_val[near, :] += jnp.dot(probs_low, do, preferred_element_type=jnp.float32)
            delta = jnp.sum(probs * d_probs, axis=0, keepdims=True)
            d_scores = (probs * (d_probs - delta) * factor).astype(jnp.bfloat16)
            d_key[near, :] += jnp.dot(d_scores, qn, preferred_element_type=jnp.float32)
            turned = jnp.dot(k_turned[:, near], d_scores, preferred_element_type=jnp.float32)
            back = turned.T * q_gain[...]
            u = q_unit[rows, :]
            d_query = q_rate[rows, :] * (back - u * jnp.mean(back * u, axis=-1, keepdims=True))
            d_joined[rows, 0:width] = d_query.astype(jnp.bfloat16)
        if i > 0:
            rows = pl.ds((i - 1) * BLOCK, BLOCK)
            back = d_key[rows, :] * k_gain[...]
            u = k_unit[rows, :]
            d_keys = k_rate[rows, :] * (back - u * jnp.mean(back * u, axis=-1, keepdims=True))
            d_joined[rows, width : 2 * width] = d_keys.astype(jnp.bfloat16)
            d_joined[rows, 2 * width :] = d_val[rows, :].astype(jnp.bfloat16)
            d_scaled[rows, :] = (d_joined[rows, :].astype(jnp.float32) * x_scale[rows, :]).astype(jnp.bfloat16)
            made[rows, :] = contract(d_joined[rows, :], proj[...], 1, 1).astype(jnp.bfloat16)
            copy = pltpu.make_async_copy(made.at[rows, :], term.at[rows, :], sems.at[i - 1])
            copy.start()
            copies.append(copy)
    for copy in copies:
        copy.wait()


def head_backward(blocks, weights, segments, q_scale, k_scale):
    tokens, features = segments.shape[0], blocks.shape[2]
    width = q_scale.shape[0]
    here = pl.BlockSpec(memory_space=pltpu.VMEM)
    low = jnp.bfloat16

    def kept(columns, dtype):
        return pltpu.VMEM((tokens, columns), dtype)

    return pl.pallas_call(
        head_kernel,
        out_shape=tuple(
            jax.ShapeDtypeStruct(shape, low) for shape in ((tokens, features), (tokens, 3 * width), (width, tokens))
        ),
        in_specs=[here] * 6,
        out_specs=(pl.BlockSpec(memory_space=pl.ANY), here, here),
        scratch_shapes=[
            pltpu.VMEM((features, 3 * width), low), pltpu.VMEM((width, features), low), kept(features, low),
            kept(3 * width, low),
            pltpu.SemaphoreType.DMA((tokens // BLOCK,)),
            kept(width, jnp.float32), kept(width, jnp.float32), kept(1, jnp.float32), kept(1, jnp.float32),
            kept(width, low), kept(width, low), kept(width, low), kept(width, low),
            kept(width, jnp.float32), kept(width, jnp.float32),
            pltpu.VMEM((width, tokens), low), pltpu.VMEM((width, tokens), low),
            kept(1, jnp.float32), kept(1, jnp.float32),
        ],
        compiler_params=pltpu.CompilerParams(vmem_limit_bytes=48 * 1024 * 1024),
        cost_estimate=pl.CostEstimate(flops=5_000_000_000, bytes_accessed=12_000_000, transcendentals=1_000_000),
    )(
        blocks, weights, segments[:, None], segments[None, :], q_scale[None, :], k_scale[None, :]
    )


def per_device(saved_input, grad_in, segment_ids, w_qkv, w_out, q_gain, k_gain):
    dp = lax.axis_size("dp")
    tokens, cot = saved_input[0, 0], grad_in[0, 0]
    three = w_qkv.shape[3]
    share = w_qkv.shape[1]
    here = pl.BlockSpec(memory_space=pltpu.VMEM)
    rows, features = tokens.shape
    block, weights = pl.pallas_call(
        first_kernel,
        out_shape=(
            jax.ShapeDtypeStruct((2 * rows + NOTE, features), jnp.float32),
            jax.ShapeDtypeStruct((share + w_out.shape[2] * features // three, three), jnp.bfloat16),
        ),
        in_specs=[here] * 4,
        out_specs=(here, here),
    )(tokens, cot, w_qkv[0, :, 0, :], w_out[0, 0])
    weights = lax.all_gather(weights, "dp", axis=0)
    blocks = lax.all_gather(block.astype(jnp.float16), "tensor", axis=0)
    blocks = blocks.astype(jnp.bfloat16)
    term, d_scaled, attended = head_backward(blocks, weights, segment_ids[0, 0], q_gain[0], k_gain[0])
    d_normed = lax.psum_scatter(term, "tensor", scatter_dimension=0, tiled=True)
    normed, cotangent = (blocks[:, at : at + rows].reshape(-1, features) for at in (0, rows))
    d_outw = contract(attended, cotangent, 1, 0)
    d_proj = contract(normed, d_scaled, 0, 0).astype(jnp.bfloat16)
    gradients = jnp.concatenate(
        [d_proj.reshape(dp, share, three), fold_wide(d_outw.astype(jnp.bfloat16), dp, three)], axis=1
    )
    terms = lax.all_to_all(gradients, "dp", 0, 0)
    total = jnp.sum(terms.astype(jnp.float32), axis=0).astype(jnp.bfloat16)
    sums = lax.all_to_all(jnp.broadcast_to(total[None], terms.shape), "dp", 0, 0)
    grad_qkv = sums[:, :share].reshape(dp * share, three)
    grad_wout = unfold_wide(sums[:, share:], w_out.shape[3])
    d_tokens = pl.pallas_call(
        last_kernel,
        out_shape=jax.ShapeDtypeStruct(tokens.shape, jnp.bfloat16),
        in_specs=[here] * 3,
        out_specs=here,
    )(tokens, cot, d_normed)
    passed = shifted(d_tokens, "pipe", -1)
    return passed[None, None], grad_qkv[None, :, None, :], grad_wout[None, None]


def solution(mesh):
    placed = (
        P("dp", "pipe", "tensor", None),
        P("dp", "pipe", "tensor", None),
        P("dp", "pipe", None),
        P("pipe", "dp", "tensor", None),
        P("pipe", "tensor", "dp", None),
        P("pipe", None),
        P("pipe", None),
    )
    return jax.shard_map(
        per_device,
        mesh=mesh,
        in_specs=placed,
        out_specs=(
            P("dp", "pipe", "tensor", None),
            P("pipe", None, "tensor", None),
            P("pipe", "tensor", None, None),
        ),
        check_vma=False,
    )
```
